32 devices in a mesh: batch: 8 (over z, y), tm: 4 (over x, core).
Axes of the slice: x: 2, y: 2, z: 4, core: 2. Of those that a mesh axis runs over, the one named last changes fastest.
Arguments:
- features: float32 [16, 1024, 512], P('batch', 'tm'), may hold values from -6 to 6
- dense_input: float32 [16, 1024, 2560], P('batch', 'tm'), may hold values from -6 to 6
- lengths: int32 [16], P('batch'), may hold values from 256 to 1024, as said below
- time_span: int32 [16, 2], P('batch'), may hold values from 0 to 960, as said below
- freq_span: int32 [16, 2], P('batch'), may hold values from 0 to 448, as said below
- w_first: bfloat16 [21, 512, 640], replicated, may hold values from -0.0625 to 0.0625
- w_rest: bfloat16 [4, 21, 640, 640], replicated, may hold values from -0.0546875 to 0.0546875
- w_res: bfloat16 [2560, 640], replicated, may hold values from -0.125 to 0.125
- norm_gains: float32 [6, 640], replicated, may hold values from 0.5 to 1.5
- norm_biases: float32 [6, 640], replicated, may hold values from -0.5 to 0.5
- cotangent: float32 [16, 1024, 640], P('batch', 'tm'), may hold values from -8 to 8
Outputs:
- result: float32 [16, 1024, 640], P('batch', 'tm')
- grad_features: float32 [16, 1024, 512], P('batch', 'tm')
- grad_dense: float32 [16, 1024, 2560], P('batch', 'tm')
- grad_first: float32 [21, 512, 640], P(None, 'tm', 'batch')
- grad_rest: float32 [4, 21, 640, 640], P(None, None, 'tm', 'batch')
- grad_res: float32 [2560, 640], P('tm', 'batch')
- grad_gains: float32 [6, 640], replicated
- grad_biases: float32 [6, 640], replicated
The draws below stay inside these ranges and needn't reach their ends.
Inputs may be any that keep to these rules, and one draw needn't show every extreme that they name: `lengths`: of each 2 consecutive utterances one has all 1024 frames; every utterance has 256 frames or more. `time_span`: column 0 is the first masked frame, column 1 the mask's width, 1 to 64. `freq_span`: column 0 is the first masked channel, column 1 the mask's width, 1 to 64.
All inputs are finite; a program needn't handle non-finite values.
Results may differ from the reference program's by a relative error of at most 0.023.
Values may be sent and summed in bfloat16 or wider, within the bound.
No kernel may reach another device: no remote copies, remote signals or barrier semaphores. Data moves between devices by JAX's collectives and lax.ppermute only.
A program may use at most 512 MiB of HBM per device.

```python
import jax
import jax.numpy as jnp
from jax import lax

C_IN = 512
C = 640
C_DENSE = 2560
KERNEL = 21
SUBS = 5
FRAMES = 1024
TSPAN = 64
FSPAN = 64
UTT_DEV = 2
UTTS = 16


def draw_lengths(key, part):
    key = jax.random.fold_in(key, 11)
    key_len, key_pick = jax.random.split(key)
    random_len = jax.random.randint(key_len, (UTTS,), FRAMES // 4, FRAMES + 1)
    chosen = jax.random.randint(key_pick, (UTTS // UTT_DEV,), 0, UTT_DEV)
    position = jnp.arange(UTTS, dtype=jnp.int32) % UTT_DEV
    is_full = position == jnp.repeat(chosen, UTT_DEV)
    return jnp.where(is_full, FRAMES, random_len).astype(jnp.int32)


def draw_spans(key, extent, most_width):
    key_start, key_width = jax.random.split(key)
    begins = jax.random.randint(key_start, (UTTS, 1), 0, extent - most_width + 1)
    widths = jax.random.randint(key_width, (UTTS, 1), 1, most_width + 1)
    return jnp.concatenate([begins, widths], axis=1).astype(jnp.int32)


def draw_time_span(key, part):
    key = jax.random.fold_in(key, 23)
    return draw_spans(key, FRAMES, TSPAN)


def draw_freq_span(key, part):
    key = jax.random.fold_in(key, 37)
    return draw_spans(key, C_IN, FSPAN)


def spiked(values, own_key, source, target, parts, factor):
    owner, partner = [(jnp.arange(values.shape[dim]) // (values.shape[dim] // parts)).reshape([-1 if axis == dim else 1 for axis in range(values.ndim)]) for dim in (source, target)]
    chosen = jax.random.permutation(own_key, parts)[partner]
    strong = (owner == chosen) | (owner == (partner + parts // 2) % parts)
    return jnp.where(strong, factor * values, values)


def steps_of(rng, dims, cuts, smallest, top_value):
    loudness, own = 1.0, jax.random.fold_in(rng, 6)
    for dim, shards_of in cuts:
        steps = jnp.exp(jax.random.uniform(jax.random.fold_in(own, dim), (shards_of,), jnp.float32, smallest / len(cuts), top_value / len(cuts)))
        loudness = loudness * jnp.repeat(steps, dims[dim] // shards_of).reshape([-1 if axis == dim else 1 for axis in range(len(dims))])
    return loudness


def noise(key, shape, width, reach, shards=(), held_as=jnp.bfloat16):
    array = jax.random.normal(key, shape, jnp.float32) * width
    if len(shards) > 0:
        array = steps_of(key, shape, shards, -0.22, 0.18) * array
    return jnp.clip(array, min=-reach, max=reach).astype(held_as)


def gaussian_with(own_key, dims, scale, reach, shards, heavy, held_as=jnp.bfloat16):
    values = scale * jax.random.normal(own_key, dims, jnp.float32)
    if shards:
        values = values * steps_of(own_key, dims, shards, -0.22, 0.18)
    return jnp.clip(spiked(values, jax.random.fold_in(own_key, 3), *heavy), -reach, reach).astype(held_as)


def setup_inputs(seed: int = 0) -> dict:
    key_of = jax.random.split(jax.random.key(seed), 12)
    features = noise(key_of[0], (UTTS, FRAMES, C_IN), 1.0, 6.0, ((0, 8), (1, 4)), jnp.float32)
    dense_input = noise(key_of[1], (UTTS, FRAMES, C_DENSE), 1.0, 6.0, ((0, 8), (1, 4)), jnp.float32)
    lengths = draw_lengths(jax.random.fold_in(key_of[11], 71), 0)
    time_span = draw_time_span(jax.random.fold_in(key_of[11], 71), 0)
    freq_span = draw_freq_span(jax.random.fold_in(key_of[11], 71), 0)
    w_first = noise(key_of[5], (KERNEL, C_IN, C), (KERNEL * C_IN) ** -0.5, 0.0625)
    w_rest = noise(key_of[6], (SUBS - 1, KERNEL, C, C), (KERNEL * C) ** -0.5, 0.0546875)
    w_res = noise(key_of[7], (C_DENSE, C), C_DENSE ** -0.5, 0.125)
    norm_gains = jnp.clip(jax.random.uniform(key_of[8], (SUBS + 1, C), jnp.float32, 0.5, 1.5), 0.5, 1.5)
    norm_biases = jnp.clip(jax.random.uniform(key_of[9], (SUBS + 1, C), jnp.float32, -0.5, 0.5), -0.5, 0.5)
    cotangent = gaussian_with(key_of[10], (UTTS, FRAMES, C), 1.0, 8.0, ((0, 8), (1, 4)), (0, 2, 8, 2.0), jnp.float32)
    return dict(features=features, dense_input=dense_input, lengths=lengths, time_span=time_span, freq_span=freq_span, w_first=w_first, w_rest=w_rest, w_res=w_res, norm_gains=norm_gains, norm_biases=norm_biases, cotangent=cotangent)


EPSILON = 1e-05

@jax.custom_vjp
def low(v):
    return lax.optimization_barrier(v.astype(jnp.bfloat16)).astype(jnp.float32)

@jax.custom_vjp
def low_back(v):
    return v

def low_keep(v):
    return (low(v), None)

def low_pass(kept, grad):
    return (grad,)

def back_keep(v):
    return (v, None)

def back_low(kept, grad):
    return (low(grad),)
low.defvjp(low_keep, low_pass)
low_back.defvjp(back_keep, back_low)

def span_keep(span_cols, extent):
    positions = jnp.arange(extent, dtype=jnp.int32)[None, :]
    inside = (positions >= span_cols[:, 0:1]) & (positions < span_cols[:, 0:1] + span_cols[:, 1:2])
    return 1.0 - inside.astype(jnp.float32)

def convolve(hidden, weight):
    half_kernel = KERNEL // 2
    padded = jnp.pad(hidden, ((0, 0), (half_kernel, half_kernel), (0, 0)))
    total = None
    for tap_index in range(KERNEL):
        term = jnp.einsum('uti,ic->utc', padded[:, tap_index:tap_index + FRAMES], weight[tap_index], precision=lax.Precision.HIGHEST)
        total = term if total is None else total + term
    return total

def normalize(linear, valid_mask, counted, gain_row, bias_row):
    average = lax.optimization_barrier(jnp.sum(linear * valid_mask, axis=(0, 1))) / counted
    square = lax.optimization_barrier(jnp.sum(linear * linear * valid_mask, axis=(0, 1))) / counted
    inv_std = lax.rsqrt(square - average * average + EPSILON)
    return (linear - average) * inv_std * gain_row + bias_row

def reference(features, dense_input, lengths, time_span, freq_span, w_first, w_rest, w_res, norm_gains, norm_biases, cotangent):
    positions = jnp.arange(FRAMES, dtype=jnp.int32)[None, :]
    valid_mask = (positions < lengths[:, None]).astype(jnp.float32)[:, :, None]
    keep_mask = valid_mask * span_keep(time_span, FRAMES)[:, :, None] * span_keep(freq_span, C_IN)[:, None, :]
    counted = jnp.sum(valid_mask)

    def forward(features, dense_input, w_first, w_rest, w_res, norm_gains, norm_biases):
        hidden = low(features * keep_mask)
        normed = None
        for sub_block in range(SUBS):
            weight = w_first if sub_block == 0 else w_rest[sub_block - 1]
            linear = low_back(convolve(hidden, weight))
            normed = normalize(linear, valid_mask, counted, norm_gains[sub_block], norm_biases[sub_block])
            if sub_block + 1 < SUBS:
                hidden = low(jax.nn.silu(normed) * valid_mask)
        branch = low_back(jnp.einsum('utd,dc->utc', low(dense_input * valid_mask), w_res, precision=lax.Precision.HIGHEST))
        joined = normed + normalize(branch, valid_mask, counted, norm_gains[SUBS], norm_biases[SUBS])
        return jax.nn.silu(joined) * valid_mask
    result, pullback = jax.vjp(forward, features, dense_input, w_first.astype(jnp.float32), w_rest.astype(jnp.float32), w_res.astype(jnp.float32), norm_gains, norm_biases)
    gradients = pullback(cotangent)
    return (result, gradients[0], gradients[1], gradients[2], gradients[3], gradients[4], gradients[5], gradients[6])
```

```python
import functools
import math

import jax
import jax.numpy as jnp
from jax import lax
from jax.experimental import pallas as pl
from jax.experimental.pallas import tpu as pltpu
from jax.sharding import Mesh, PartitionSpec as P

EPSILON = 1e-05
ALL = ("zh", "zl", "y", "x", "core")
DEPTH = ("zh", "zl")
BATCH = ("zh", "zl", "y")
TIME = ("x", "core")
LANES = 128
GROUP = 7
VMEM = pl.BlockSpec(memory_space=pltpu.VMEM)
SMEM = pl.BlockSpec(memory_space=pltpu.SMEM)
ANY = pl.BlockSpec(memory_space=pl.ANY)
PARAMS = pltpu.CompilerParams(vmem_limit_bytes=60 * 1024 * 1024)


def pieces_of(count):
    return -(-count // (8 * LANES)) * 8


def silu_slope(hidden):
    logistic = jax.nn.sigmoid(hidden)
    return logistic * (1.0 + hidden * (1.0 - logistic))


def plan(utterances, rows, kernel_len):
    phases = rows // LANES
    half = kernel_len // 2
    blocks = []
    for q in range(phases + kernel_len - 1):
        move = (q - half) // phases
        blocks.append((q - half - move * phases, move))
    reach = max(abs(move) for _, move in blocks)
    edge = -(-reach * utterances // 8) * 8
    return phases, blocks, edge


def valid_of(info, utterances, phases, phase, first, shape, axis):
    row = lax.broadcasted_iota(jnp.int32, shape, axis) + first
    frame = info[utterances] + (row // utterances) * phases + phase
    which = row % utterances
    length = jnp.full(shape, info[0], jnp.int32)
    for u in range(1, utterances):
        length = jnp.where(which == u, info[u], length)
    return ((frame >= 0) & (frame < length)).astype(jnp.float32)


def spread_blocks(blocks, utterances, axis, own, edges, put):
    for q, (phase, move) in enumerate(blocks):
        block = own[phase]
        if move:
            spot = lax.broadcasted_iota(jnp.int32, block.shape, axis)
            if move > 0:
                outside = spot < move * utterances
            else:
                outside = spot >= LANES + move * utterances
            block = jnp.where(outside, edges[phase], block)
            block = pltpu.roll(block, (-move * utterances) % LANES, axis)
        put(q, block)


def fetch(weight, base, buffer, sems, g):
    return pltpu.make_async_copy(weight.at[base + g], buffer.at[g], sems.at[g])


def flat_sums(came):
    summed = jnp.sum(came, axis=0)
    return jnp.concatenate([summed[i : i + 1] for i in range(summed.shape[0])], axis=1)


def put_sums(sums, rows_list):
    copies, pieces, _ = sums.shape
    at = 0
    for row in rows_list:
        for i in range(row.shape[1] // LANES):
            piece = row[:, i * LANES : (i + 1) * LANES]
            sums[:, at, :] = jnp.broadcast_to(piece, (copies, LANES))
            at += 1
    if at < pieces:
        sums[:, at:, :] = jnp.zeros((copies, pieces - at, LANES), jnp.float32)


def norm_terms(came, cout):
    summed = flat_sums(came)
    counted = summed[:, 2 * cout : 2 * cout + 1]
    average = summed[:, :cout] / counted
    inv = lax.rsqrt(summed[:, cout : 2 * cout] / counted - average * average + EPSILON)
    return average, inv, counted


def span_of(info, utterances, phases, phase, which, shape):
    at = utterances + 2 + 4 * which
    frame = info[utterances] + lax.broadcasted_iota(jnp.int32, shape, 0) * phases + phase
    channel = lax.broadcasted_iota(jnp.int32, shape, 1)
    inside = (frame >= info[at]) & (frame < info[at] + info[at + 1])
    inside |= (channel >= info[at + 2]) & (channel < info[at + 2] + info[at + 3])
    return ((frame < info[which]) & jnp.logical_not(inside)).astype(jnp.float32)


def frames_of(utterances, phases, phase, which):
    count = LANES // utterances
    return pl.ds(which * count * phases + phase, count, stride=phases)


def rows_of(utterances, first, which):
    return pl.ds(first + which, LANES // utterances, stride=utterances)


def lay(ref, stage):
    for j in range(stage.shape[0]):
        stage[j] = ref[:, j * LANES : (j + 1) * LANES]


def unlay(stage, ref):
    for j in range(stage.shape[0]):
        ref[:, j * LANES : (j + 1) * LANES] = stage[j]


def take(stage, index):
    return jnp.concatenate([stage[j, index, :] for j in range(stage.shape[0])], axis=1)


def give(stage, index, value):
    for j in range(stage.shape[0]):
        stage[j, index, :] = value[:, j * LANES : (j + 1) * LANES]


def forward_kernel(
    cfg, info, source, low, high, came, gain, bias, more, weight, linear, sums, low_out, high_out, flat, turned,
    buffer, haloed, sems, laid, staged,
):
    utterances, phases, blocks, edge, taps, base, normed = cfg
    groups = taps // GROUP
    rows, cin = source.shape
    cout = linear.shape[1]
    fetch(weight, base, buffer, sems, 0).start()
    if normed:
        average, inv, _ = norm_terms(came[...], cin)
        scale = inv * gain[...]
        shift = bias[...] - average * scale

    else:
        lay(source, laid)

    def activate(value, mask):
        if not normed:
            return value.astype(jnp.float32)
        value = value * scale + shift
        return value * jax.nn.sigmoid(value) * mask

    own, edges = [], []
    for p in range(phases):
        if normed:
            mask = valid_of(info, utterances, phases, p, 0, (LANES, 1), 0)
            block = activate(source[p * LANES : (p + 1) * LANES, :], mask).astype(jnp.bfloat16)
        else:
            for u in range(utterances):
                mask = span_of(info, utterances, phases, p, u, (LANES // utterances, cin))
                give(staged, rows_of(utterances, 0, u), take(laid, frames_of(utterances, phases, p, u)) * mask)
            block = take(staged, slice(None)).astype(jnp.bfloat16)
        own.append(block)
        flat[:, p * LANES : (p + 1) * LANES] = block.T
        mask = valid_of(info, utterances, phases, p, -edge, (edge, 1), 0)
        before = activate(low[p], mask)
        mask = valid_of(info, utterances, phases, p, LANES, (edge, 1), 0)
        after = activate(high[p], mask)
        middle = jnp.zeros((LANES - 2 * edge, cin), jnp.float32)
        edges.append(jnp.concatenate([after, middle, before], axis=0).astype(jnp.bfloat16))

    def put(q, block):
        haloed[q * LANES : (q + 1) * LANES, :] = block

    if groups > 1:
        fetch(weight, base, buffer, sems, 1).start()
    spread_blocks(blocks, utterances, 0, own, edges, put)
    linear[...] = jnp.zeros_like(linear)

    def step(g, carry):
        fetch(weight, base, buffer, sems, g).wait()

        @pl.when(g + 2 < groups)
        def _():
            fetch(weight, base, buffer, sems, g + 2).start()

        lhs = jnp.concatenate(
            [
                haloed[pl.ds(pl.multiple_of((g * GROUP + k) * LANES, LANES), rows), :]
                for k in range(GROUP)
            ],
            axis=1,
        )
        linear[...] += jnp.dot(lhs, buffer[g], preferred_element_type=jnp.float32)
        return carry

    lax.fori_loop(0, groups, step, 0)
    total = jnp.zeros((1, cout), jnp.float32)
    square = jnp.zeros((1, cout), jnp.float32)
    count = jnp.zeros((1, 1), jnp.float32)
    for p in range(phases):
        mask = valid_of(info, utterances, phases, p, 0, (LANES, 1), 0)
        block = linear[p * LANES : (p + 1) * LANES, :]
        masked = block * mask
        total += jnp.sum(masked, axis=0, keepdims=True)
        square += jnp.sum(masked * block, axis=0, keepdims=True)
        count += jnp.sum(mask, axis=0, keepdims=True)
        low_out[p] = block[LANES - edge :, :]
        high_out[p] = block[:edge, :]
        turned[:, p * LANES : (p + 1) * LANES] = block.astype(jnp.bfloat16).T
    terms = [total, square, jnp.broadcast_to(count, (1, LANES))]
    if more is not None:
        terms.append(more[...])
    put_sums(sums, terms)


def forward_conv(utterances, info, source, low, high, came, gain, bias, weight, layer, copies, more=None):
    _, taps, cin, cout = weight.shape
    rows = source.shape[0]
    phases, blocks, edge = plan(utterances, rows, taps)
    groups = taps // GROUP
    normed = came is not None
    if not normed:
        came = jnp.zeros((1, 8, LANES), jnp.float32)
        gain = bias = jnp.zeros((1, LANES), jnp.float32)
    cfg = (utterances, phases, blocks, edge, taps, layer * groups, normed)
    shape = jax.ShapeDtypeStruct
    terms = 2 * cout + LANES
    kernel = functools.partial(forward_kernel, cfg)
    extra = []
    if more is None:
        kernel = lambda *refs: forward_kernel(cfg, *refs[:7], None, *refs[7:])
    else:
        terms += more.shape[1]
        extra = [more]
    return pl.pallas_call(
        kernel,
        name="forward_conv",
        out_shape=(
            shape((rows, cout), jnp.float32),
            shape((copies, pieces_of(terms), LANES), jnp.float32),
            shape((phases, edge, cout), jnp.float32),
            shape((phases, edge, cout), jnp.float32),
            shape((cin, rows), jnp.bfloat16),
            shape((cout, rows), jnp.bfloat16),
        ),
        in_specs=[SMEM] + [VMEM] * (6 + len(extra)) + [ANY],
        out_specs=(VMEM,) * 6,
        scratch_shapes=[
            pltpu.VMEM((groups, GROUP * cin, cout), jnp.bfloat16),
            pltpu.VMEM((len(blocks) * LANES, cin), jnp.bfloat16),
            pltpu.SemaphoreType.DMA((groups,)),
            pltpu.VMEM((1 if normed else cin // LANES, 8 if normed else rows, LANES), jnp.float32),
            pltpu.VMEM((cin // LANES, LANES, LANES), jnp.float32),
        ],
        compiler_params=PARAMS,
        cost_estimate=pl.CostEstimate(
            flops=2 * taps * rows * cin * cout, bytes_accessed=2 * taps * cin * cout, transcendentals=0
        ),
    )(info, source, low, high, came, gain, bias, *extra, weight.reshape(-1, GROUP * cin, cout))


def columns_of(rows_list):
    count = len(rows_list)
    width = rows_list[0].shape[1]
    stacked = jnp.concatenate(
        rows_list + [jnp.zeros((LANES - count, width), jnp.float32)], axis=0
    )
    return stacked.T


def put_grad(out, value, table):
    if len(out.shape) == 2:
        out[...] = value
        return
    cols = out.shape[3]
    for g, blocks in enumerate(table):
        for k, block in enumerate(blocks):
            for x in range(out.shape[1]):
                out[g, x, k] = value[block * cols : (block + 1) * cols]


def backward_kernel(
    cfg, info, up, linear, low_up, high_up, low_lin, high_lin, came, came_up, gain, before, came_before,
    gain_before, bias_before, weight, grad, next_up, sums, low_out, high_out, row, buffer, haloed, sems, staged,
    whole, laid,
):
    utterances, phases, blocks, edge, taps, base, last, table = cfg
    groups = taps // GROUP
    cout, rows = up.shape
    cin = weight.shape[2]
    fetch(weight, base, buffer, sems, 0).start()
    average, inv, counted = norm_terms(came[...], cout)
    summed = flat_sums(came_up[...])
    grad_gain, grad_bias = summed[:, :cout], summed[:, cout : 2 * cout]
    row[...] = summed[:, : 2 * cout]
    keep_up = gain[...] * inv
    keep_lin = -keep_up * inv * grad_gain / counted
    rest = -keep_up * grad_bias / counted - keep_lin * average
    vectors = [keep_up, keep_lin, rest]
    if not last:
        average_b, inv_b, _ = norm_terms(came_before[...], cin)
        scale = inv_b * gain_before[...]
        vectors += [scale, bias_before[...] - average_b * scale, inv_b, -average_b * inv_b]
    columns = columns_of(vectors)

    def column(r):
        return columns[:, r : r + 1]

    pieces = []
    for p in range(phases):
        for first, up_edge, lin_edge in ((-edge, low_up, low_lin), (LANES, high_up, high_lin)):
            mask = valid_of(info, utterances, phases, p, first, (edge, 1), 0)
            pieces.append(mask * (up_edge[p] * keep_up + lin_edge[p] * keep_lin + rest))
    pieces.append(jnp.zeros((LANES - 2 * phases * edge, cout), jnp.float32))
    side = jnp.concatenate(pieces, axis=0).T
    own, edges, grads = [], [], []
    spot = lax.broadcasted_iota(jnp.int32, (cout, LANES), 1)
    for p in range(phases):
        cut = slice(p * LANES, (p + 1) * LANES)
        mask = valid_of(info, utterances, phases, p, 0, (1, LANES), 1)
        block = mask * (up[:, cut] * column(0) + linear[:, cut].astype(jnp.float32) * column(1) + column(2))
        block = block.astype(jnp.bfloat16)
        own.append(block)
        grads.append(block)
        at = 2 * p * edge
        after = pltpu.roll(side, (-(at + edge)) % LANES, 1)
        ahead = pltpu.roll(side, (LANES - edge - at) % LANES, 1)
        edges.append(jnp.where(spot < edge, after, ahead).astype(jnp.bfloat16))

    put_grad(grad, jnp.concatenate(grads, axis=1), table)

    def put(q, block):
        haloed[:, q * LANES : (q + 1) * LANES] = block

    if groups > 1:
        fetch(weight, base, buffer, sems, 1).start()
    spread_blocks(blocks, utterances, 1, own, edges, put)
    total = whole if last else next_up
    for g in range(groups):
        fetch(weight, base, buffer, sems, g).wait()
        if g + 2 < groups:
            fetch(weight, base, buffer, sems, g + 2).start()
        lhs = jnp.concatenate([buffer[g, k] for k in range(GROUP)], axis=1)
        starts = [(taps - 1 - g * GROUP - k) * LANES for k in range(GROUP)]
        rhs = jnp.concatenate([haloed[:, at : at + rows] for at in starts], axis=0)
        product = jnp.dot(lhs, rhs, preferred_element_type=jnp.float32)
        total[...] = product if g == 0 else total[...] + product
    if last:
        for p in range(phases):
            give(staged, slice(None), total[:, p * LANES : (p + 1) * LANES].T)
            for u in range(utterances):
                mask = span_of(info, utterances, phases, p, u, (LANES // utterances, cin))
                give(laid, frames_of(utterances, phases, p, u), take(staged, rows_of(utterances, 0, u)) * mask)
        unlay(laid, next_up)
        return
    gains = jnp.zeros((cin, LANES), jnp.float32)
    biases = jnp.zeros((cin, LANES), jnp.float32)
    ends = jnp.zeros((cin, LANES), jnp.float32)
    spot = lax.broadcasted_iota(jnp.int32, (cin, LANES), 1)
    for p in range(phases):
        cut = slice(p * LANES, (p + 1) * LANES)
        mask = valid_of(info, utterances, phases, p, 0, (1, LANES), 1)
        value = before[:, cut].astype(jnp.float32)
        block = next_up[:, cut] * mask * silu_slope(value * column(3) + column(4))
        next_up[:, cut] = block
        gains += block * (value * column(5) + column(6))
        biases += block
        at = 2 * p * edge
        rolled = pltpu.roll(block, (at + edge) % LANES, 1)
        ends = jnp.where((spot >= at) & (spot < at + 2 * edge), rolled, ends)
    ends = ends.T
    for p in range(phases):
        at = 2 * p * edge
        low_out[p] = ends[at : at + edge, :]
        high_out[p] = ends[at + edge : at + 2 * edge, :]
    gains = jnp.sum(gains.T, axis=0, keepdims=True)
    biases = jnp.sum(biases.T, axis=0, keepdims=True)
    put_sums(sums, [gains, biases])


def backward_conv(
    utterances, info, up, linear, low_up, high_up, low_lin, high_lin, came, came_up, gain, before, came_before,
    gain_before, bias_before, weight, layer, copies, split, table,
):
    _, taps, cin, cout = weight.shape
    rows = up.shape[1]
    phases, blocks, edge = plan(utterances, rows, taps)
    groups = taps // GROUP
    last = before is None
    if last:
        before = jnp.zeros((16, LANES), jnp.bfloat16)
        came_before = jnp.zeros((1, 8, LANES), jnp.float32)
        gain_before = bias_before = jnp.zeros((1, LANES), jnp.float32)
    shape = jax.ShapeDtypeStruct
    cfg = (utterances, phases, blocks, edge, taps, layer * groups, last, table)
    return pl.pallas_call(
        functools.partial(backward_kernel, cfg),
        name="backward_conv",
        out_shape=(
            shape(split + (rows,), jnp.bfloat16),
            shape((rows, cin) if last else (cin, rows), jnp.float32),
            shape((copies, pieces_of(2 * cin), LANES), jnp.float32),
            shape((phases, edge, cin), jnp.float32),
            shape((phases, edge, cin), jnp.float32),
            shape((1, 2 * cout), jnp.float32),
        ),
        in_specs=[SMEM] + [VMEM] * 13 + [ANY],
        out_specs=(VMEM,) * 6,
        scratch_shapes=[
            pltpu.VMEM((groups, GROUP, cin, cout), jnp.bfloat16),
            pltpu.VMEM((cout, len(blocks) * LANES), jnp.bfloat16),
            pltpu.SemaphoreType.DMA((groups,)),
            pltpu.VMEM((cin // LANES, LANES, LANES), jnp.float32),
            pltpu.VMEM((cin, rows) if last else (8, LANES), jnp.float32),
            pltpu.VMEM((cin // LANES, rows, LANES) if last else (1, 8, LANES), jnp.float32),
        ],
        compiler_params=PARAMS,
        cost_estimate=pl.CostEstimate(
            flops=2 * taps * rows * cin * cout, bytes_accessed=2 * taps * cin * cout, transcendentals=0
        ),
    )(
        info, up, linear, low_up, high_up, low_lin, high_lin, came, came_up, gain, before, came_before,
        gain_before, bias_before, weight.reshape(-1, GROUP, cin, cout),
    )


def weight_kernel(cfg, info, hidden_all, *refs):
    utterances, phases, blocks, taps, batch, first, parts = cfg
    pieces, (out, hidden, grad, haloed, total, sems) = refs[:parts], refs[parts:]
    inner, width, cin, rows = hidden.shape
    cout = grad.shape[2]
    across = width // parts

    def copies_of(b):
        for p, piece in enumerate(pieces):
            for x in range(across):
                at = (p * inner + b) * across + x
                yield pltpu.make_async_copy(piece.at[b * across + x], grad.at[at], sems.at[at])
        source = hidden_all.at[b, :, pl.ds(first, cin), :]
        yield pltpu.make_async_copy(source, hidden.at[b], sems.at[width * inner + b])

    def start(b, carry):
        for copy in copies_of(b):
            copy.start()
        return carry

    lax.fori_loop(0, inner, start, 0)
    total[...] = jnp.zeros_like(total)
    zero = jnp.zeros((cin, LANES), hidden.dtype)
    spot = lax.broadcasted_iota(jnp.int32, (cin, LANES), 1)

    def unit(b, carry):
        for copy in copies_of(b):
            copy.wait()
        for t in range(width):
            for q, (phase, move) in enumerate(blocks):
                cut = slice(phase * LANES, (phase + 1) * LANES)
                block = hidden[b, t, :, cut]
                if move:
                    if move > 0:
                        other = hidden[b, t + 1, :, cut] if t + 1 < width else zero
                        outside = spot < move * utterances
                    else:
                        other = hidden[b, t - 1, :, cut] if t > 0 else zero
                        outside = spot >= LANES + move * utterances
                    block = pltpu.roll(jnp.where(outside, other, block), (-move * utterances) % LANES, 1)
                haloed[t, :, q * LANES : (q + 1) * LANES] = block
        lhs = jnp.concatenate(
            [grad[(p * inner + b) * across + x] for p in range(parts) for x in range(across)], axis=1
        )

        places = [x * parts + jnp.bitwise_xor(info[0], p) for p in range(parts) for x in range(across)]
        for g in range(taps // batch):
            rhs = jnp.concatenate(
                [
                    jnp.concatenate([haloed[place, :, k * LANES : k * LANES + rows] for place in places], axis=1)
                    for k in range(g * batch, (g + 1) * batch)
                ],
                axis=0,
            )
            total[g] += lax.dot_general(
                lhs, rhs, (((1,), (1,)), ((), ())), preferred_element_type=jnp.float32
            )
        return carry

    lax.fori_loop(0, inner, unit, 0)
    outer, _, cols, _ = out.shape
    for z in range(outer):
        out[z] = total[:, z * cols : (z + 1) * cols, :].astype(jnp.bfloat16)


def weight_grad(utterances, taps, order, hidden, first, cin, grad, outer):
    inner, width, _, rows = hidden.shape
    cout = grad[0].shape[1]
    phases, blocks, _ = plan(utterances, rows, taps)
    batch = 7
    cfg = (utterances, phases, blocks, taps, batch, first, len(grad))
    return pl.pallas_call(
        functools.partial(weight_kernel, cfg),
        name="weight_grad",
        out_shape=jax.ShapeDtypeStruct((outer, taps // batch, cout // outer, batch * cin), jnp.bfloat16),
        in_specs=[SMEM] + [ANY] * (1 + len(grad)),
        out_specs=VMEM,
        scratch_shapes=[
            pltpu.VMEM((inner, width, cin, rows), jnp.bfloat16),
            pltpu.VMEM((width * inner, cout, rows), jnp.bfloat16),
            pltpu.VMEM((width, cin, len(blocks) * LANES), jnp.bfloat16),
            pltpu.VMEM((taps // batch, cout, batch * cin), jnp.float32),
            pltpu.SemaphoreType.DMA((inner + width * inner,)),
        ],
        compiler_params=PARAMS,
        cost_estimate=pl.CostEstimate(
            flops=2 * taps * inner * width * rows * cin * cout,
            bytes_accessed=2 * inner * width * rows * (cin + cout),
            transcendentals=0,
        ),
    )(order, hidden, *grad)


def branch_terms(first, second, counted, channels):
    at = 2 * channels + LANES
    average = flat_sums(first[...])[:, at : at + channels] / counted
    square = flat_sums(second[...])[:, at : at + channels] / counted
    return average, lax.rsqrt(square - average * average + EPSILON)


def middle_kernel(
    cfg, info, linear, came, first, second, branch, cotangent, gain, bias, branch_gain, branch_bias, result, up, turned, sums,
    low_out, high_out, staged, linear_laid, branch_laid, cotangent_laid, result_laid, up_laid,
):
    utterances, phases, edge = cfg
    channels = linear.shape[1]
    average, inv, counted = norm_terms(came[...], channels)
    branch_average, branch_inv = branch_terms(first, second, counted, channels)
    zero = jnp.zeros((1, channels), jnp.float32)
    gain_sum, bias_sum, branch_sum = zero, zero, zero
    lay(linear, linear_laid)
    lay(branch, branch_laid)
    lay(cotangent, cotangent_laid)
    shape = (LANES // utterances, 1)
    for p in range(phases):
        for u in range(utterances):
            here = frames_of(utterances, phases, p, u)
            frame = info[utterances] + lax.broadcasted_iota(jnp.int32, shape, 0) * phases + p
            mask = (frame < info[u]).astype(jnp.float32)
            scaled = (take(linear_laid, rows_of(utterances, p * LANES, u)) - average) * inv
            branch_scaled = (take(branch_laid, here) - branch_average) * branch_inv
            joined = scaled * gain[...] + bias[...] + (branch_scaled * branch_gain[...] + branch_bias[...])
            logistic = jax.nn.sigmoid(joined)
            give(result_laid, here, joined * logistic * mask)
            grad = take(cotangent_laid, here) * mask * (logistic * (1.0 + joined * (1.0 - logistic)))
            give(up_laid, here, grad)
            give(staged, rows_of(utterances, 0, u), grad)
            gain_sum += jnp.sum(grad * scaled, axis=0, keepdims=True)
            bias_sum += jnp.sum(grad, axis=0, keepdims=True)
            branch_sum += jnp.sum(grad * branch_scaled, axis=0, keepdims=True)
        block = take(staged, slice(None))
        turned[:, p * LANES : (p + 1) * LANES] = block.T
        low_out[p] = block[LANES - edge :, :]
        high_out[p] = block[:edge, :]
    unlay(result_laid, result)
    unlay(up_laid, up)
    put_sums(sums, [gain_sum, bias_sum, branch_sum])


def middle(utterances, info, linear, came, first, second, branch, cotangent, terms, edge, copies):
    rows, channels = linear.shape
    phases = rows // LANES
    shape = jax.ShapeDtypeStruct
    return pl.pallas_call(
        functools.partial(middle_kernel, (utterances, phases, edge)),
        name="middle",
        out_shape=(
            shape((rows, channels), jnp.float32),
            shape((rows, channels), jnp.float32),
            shape((channels, rows), jnp.float32),
            shape((copies, pieces_of(3 * channels), LANES), jnp.float32),
            shape((phases, edge, channels), jnp.float32),
            shape((phases, edge, channels), jnp.float32),
        ),
        in_specs=[SMEM] + [VMEM] * 10,
        out_specs=(VMEM,) * 6,
        scratch_shapes=[pltpu.VMEM((channels // LANES, LANES, LANES), jnp.float32)]
        + [pltpu.VMEM((channels // LANES, rows, LANES), jnp.float32)] * 5,
        compiler_params=PARAMS,
        cost_estimate=pl.CostEstimate(
            flops=40 * rows * channels, bytes_accessed=24 * rows * channels, transcendentals=rows * channels
        ),
    )(info, linear, came, first, second, branch, cotangent, *terms)


def residual_kernel(cfg, info, dense, branch, up, first, second, came_up, gain, grad, product):
    utterances, parts = cfg
    rows, channels = branch.shape
    total = flat_sums(came_up[...])
    counted = flat_sums(first[...])[:, 2 * channels : 2 * channels + 1]
    average, inv = branch_terms(first, second, counted, channels)
    keep_up = gain[...] * inv
    keep_branch = -keep_up * inv * total[:, 2 * channels : 3 * channels] / counted
    rest = -keep_up * total[:, channels : 2 * channels] / counted - keep_branch * average
    count = rows // utterances
    frame = info[utterances] + lax.broadcasted_iota(jnp.int32, (count, 1), 0)
    mask = jnp.concatenate([(frame < info[u]).astype(jnp.float32) for u in range(utterances)], axis=0)
    value = (mask * (up[...] * keep_up + branch[...] * keep_branch + rest)).astype(jnp.bfloat16)
    grad[...] = value
    turned = value.T
    size = dense.shape[1] // parts
    if size % LANES == 0:
        for t in range(parts):
            low = (dense[:, t * size : (t + 1) * size] * mask).astype(jnp.bfloat16)
            product[t] = jnp.dot(turned, low, preferred_element_type=jnp.float32).astype(jnp.bfloat16)
    else:
        low = (dense[...] * mask).astype(jnp.bfloat16)
        every_part = jnp.dot(turned, low, preferred_element_type=jnp.float32).astype(jnp.bfloat16)
        for t in range(parts):
            product[t] = every_part[:, t * size : (t + 1) * size]


def residual(utterances, info, dense, branch, up, first, second, came_up, gain, parts):
    rows, channels = branch.shape
    deep = dense.shape[1]
    shape = jax.ShapeDtypeStruct
    return pl.pallas_call(
        functools.partial(residual_kernel, (utterances, parts)),
        name="residual",
        out_shape=(
            shape((rows, channels), jnp.bfloat16),
            shape((parts, channels, deep // parts), jnp.bfloat16),
        ),
        in_specs=[SMEM] + [VMEM] * 7,
        out_specs=(VMEM,) * 2,
        compiler_params=PARAMS,
        cost_estimate=pl.CostEstimate(
            flops=2 * rows * channels * deep, bytes_accessed=4 * rows * deep, transcendentals=0
        ),
    )(info, dense, branch, up, first, second, came_up, gain)


def finish_kernel(cfg, *refs):
    taps, terms, turned = cfg
    parts, out = refs[:terms], refs[-1]
    groups = parts[0].shape[0]
    batch = taps // groups
    for g in range(groups):
        block = parts[0][g].astype(jnp.float32)
        for part in parts[1:]:
            block += part[g].astype(jnp.float32)
        size = block.shape[1] // batch
        if turned:
            for k in range(batch):
                out[g * batch + k] = block[:, k * size : (k + 1) * size]
        else:
            out[g * batch : (g + 1) * batch] = block.T.reshape(batch, size, block.shape[0])


def finish(taps, parts, layer=0, layers=1, buffer=None, turned=False):
    groups, cols, long = parts[0].shape
    cin = long * groups // taps
    block = (taps, cols, cin) if turned else (taps, cin, cols)
    extra = [] if buffer is None else [buffer]
    return pl.pallas_call(
        functools.partial(finish_kernel, (taps, len(parts), turned)),
        name="finish",
        grid=(1,),
        out_shape=jax.ShapeDtypeStruct((layers,) + block, jnp.float32),
        in_specs=[VMEM] * len(parts) + [ANY] * len(extra),
        out_specs=pl.BlockSpec((None,) + block, lambda i: (layer, 0, 0, 0)),
        input_output_aliases={len(parts): 0} if extra else {},
        compiler_params=PARAMS,
    )(*parts, *extra)


def span_keep(span_cols, positions):
    inside = (positions[None, :] >= span_cols[:, 0:1]) & (
        positions[None, :] < span_cols[:, 0:1] + span_cols[:, 1:2]
    )
    return 1.0 - inside.astype(jnp.float32)


def edge_rows(frames, phases):
    utterances, count, channels = frames.shape
    cut = frames.reshape(utterances, count // phases, phases, channels).transpose(2, 1, 0, 3)
    return cut.reshape(phases, utterances * count // phases, channels)


def swap_edges(low_out, high_out):
    count = lax.axis_size(TIME)
    low = lax.ppermute(low_out, TIME, [(i, i + 1) for i in range(count - 1)])
    high = lax.ppermute(high_out, TIME, [(i + 1, i) for i in range(count - 1)])
    return low, high


def every(copies):
    return lax.all_to_all(copies, ALL, split_axis=0, concat_axis=0, tiled=True)


def body(
    features,
    dense_input,
    lengths,
    time_span,
    freq_span,
    w_first,
    w_rest,
    w_res,
    norm_gains,
    norm_biases,
    cotangent,
):
    utterances, frames_here, in_channels = features.shape
    high_z, low_z, inner, across, cores = (lax.axis_size(name) for name in ALL)
    outer = high_z * low_z
    width = across * cores
    copies = outer * inner * width
    taps, _, channels = w_first.shape
    blocks = 1 + w_rest.shape[0]
    rows = utterances * frames_here
    phases, _, edge = plan(utterances, rows, taps)
    cols = channels // (outer * inner)
    late = 0
    whole_table = [[z * inner + y for z in range(outer)] for y in range(inner)]
    half_table = [
        [(h * low_z + l) * inner + y for h in range(high_z)] for l in range(low_z) for y in range(inner)
    ]
    offset = lax.axis_index(TIME) * frames_here
    spans = jnp.concatenate([time_span, freq_span], axis=1).reshape(-1)
    info = jnp.concatenate([lengths, jnp.stack([offset, 0]).astype(jnp.int32), spans])
    frames = offset + jnp.arange(frames_here, dtype=jnp.int32)
    valid = (frames[None, :] < lengths[:, None]).astype(jnp.float32)[:, :, None]
    layers = [(w_first[None], 0)] + [(w_rest, s) for s in range(blocks - 1)]
    gains = [norm_gains[s : s + 1] for s in range(blocks + 1)]
    biases = [norm_biases[s : s + 1] for s in range(blocks + 1)]

    def masked_edge(first, count):
        at = frames[first : first + count]
        keep = (at[None, :] < lengths[:, None]).astype(jnp.float32)[:, :, None]
        keep *= span_keep(time_span, at)[:, :, None]
        keep *= span_keep(freq_span, jnp.arange(in_channels, dtype=jnp.int32))[:, None, :]
        cut = (features[:, first : first + count] * keep).astype(jnp.bfloat16)
        return edge_rows(cut.astype(jnp.float32), phases)

    def spread_hidden(turned):
        cut = turned.reshape(width, turned.shape[0] // width, rows)
        return lax.all_to_all(cut, TIME, split_axis=0, concat_axis=0, tiled=True)

    def gather_hidden(near, s):
        return lax.all_gather(near, "y" if s >= late else ("zl", "y"))

    def plan_grad(s):
        table, axes = (whole_table, ("y",)) if s >= late else (half_table, ("zl", "y"))
        split = (len(table), across, len(table[0]), cols) if cols % 16 == 0 else (channels,)
        return table, split, axes + ("x",)

    def spread_grad(grad, s):
        table, _, axes = plan_grad(s)
        if grad.ndim == 2:
            cut = grad.reshape(outer * inner, cols, rows)[jnp.array(table)][:, None]
            grad = jnp.broadcast_to(cut, (len(table), across) + cut.shape[2:])
        grad = grad.reshape(len(table) * across, -1, rows)
        return lax.all_to_all(grad, axes, split_axis=0, concat_axis=0, tiled=True)

    def other_core(near):
        return lax.ppermute(near, "core", [(0, 1), (1, 0)]) if cores == 2 else None

    def grad_of_weights(hidden, near, far, s):
        pieces, order = [near], jnp.zeros((1,), jnp.int32)
        if far is not None:
            pieces.append(far)
            order = lax.axis_index("core").astype(jnp.int32)[None]
        places = outer if s >= late else high_z
        return weight_grad(utterances, taps, order, hidden, 0, hidden.shape[2], pieces, places)

    def sum_over_z_by_pairs(part):
        if (high_z, low_z) != (2, 2):
            return sum_over_z(part, 0)
        me = 2 * lax.axis_index("zh") + lax.axis_index("zl")

        def block(bits):
            return lax.dynamic_index_in_dim(part, jnp.bitwise_xor(me, bits), 0, keepdims=False)

        across = lax.ppermute(block(3), "zl", [(0, 1), (1, 0)])
        beside = lax.ppermute(block(1), "zl", [(0, 1), (1, 0)])
        both = (block(2).astype(jnp.float32) + across.astype(jnp.float32)).astype(jnp.bfloat16)
        return [block(0), beside, lax.ppermute(both, "zh", [(0, 1), (1, 0)])]

    def sum_over_z(part, s):
        if s >= late:
            return [lax.psum_scatter(part, DEPTH, scatter_dimension=0, tiled=True)[0]]
        if high_z != 2:
            return [lax.psum_scatter(part, "zh", scatter_dimension=0, tiled=True)[0]]
        me = lax.axis_index("zh")
        away = lax.dynamic_index_in_dim(part, 1 - me, 0, keepdims=False)
        came = lax.ppermute(away, "zh", [(0, 1), (1, 0)])
        own = lax.dynamic_index_in_dim(part, me, 0, keepdims=False)
        return [own, came]

    reach = edge * phases // utterances
    low, high = swap_edges(masked_edge(frames_here - reach, reach), masked_edge(0, reach))
    source = features.reshape(rows, in_channels)
    dense_low = (dense_input * valid).astype(jnp.bfloat16)
    branch = jnp.einsum("utd,dc->utc", dense_low, w_res, preferred_element_type=jnp.float32)
    branch_sums = {
        blocks - 3: jnp.sum(branch * valid, axis=(0, 1))[None],
        blocks - 2: jnp.sum(branch * branch * valid, axis=(0, 1))[None],
    }
    came_all, hidden_all, turned_all, edges_all = [], [], [], []
    came = None
    near = None
    for s in range(blocks):
        weight, layer = layers[s]
        more = branch_sums.get(s)
        source, sums, low_out, high_out, flat, turned = forward_conv(
            utterances, info, source, low, high, came, gains[s - 1], biases[s - 1], weight, layer, copies, more
        )
        if near is not None:
            done = hidden_all[: max(s - 2, 0)]
            sums, near, done = lax.optimization_barrier((sums, near, done))
            hidden_all[: len(done)] = done
            hidden_all.append(gather_hidden(near, s - 1))
        low, high = swap_edges(low_out, high_out)
        came = every(sums)
        flat, came, low, high = lax.optimization_barrier((flat, came, low, high))
        if s + 1 < blocks:
            near = spread_hidden(flat)
        came_all.append(came)
        turned_all.append(turned)
        edges_all.append((low, high))

    result, upstream, up, sums, low_out, high_out = middle(
        utterances,
        info,
        source,
        came,
        came_all[blocks - 3],
        came_all[blocks - 2],
        branch.reshape(rows, channels),
        cotangent.reshape(rows, channels),
        (gains[blocks - 1], biases[blocks - 1], gains[blocks], biases[blocks]),
        edge,
        copies,
    )
    done = hidden_all[: blocks - 2]
    sums, done = lax.optimization_barrier((sums, done))
    hidden_all[: len(done)] = done
    low_up, high_up = swap_edges(low_out, high_out)
    came_up = every(sums)
    flat, came_up, low_up, high_up = lax.optimization_barrier((flat, came_up, low_up, high_up))
    hidden_near = spread_hidden(flat)

    def row_of(terms):
        return jnp.sum(terms, axis=0).reshape(1, -1)

    total = row_of(came_up)
    gain_grads, bias_grads = [None] * (blocks + 1), [None] * (blocks + 1)
    gain_grads[blocks], bias_grads[blocks] = total[:, 2 * channels : 3 * channels], total[:, channels : 2 * channels]
    branch_grad, grad_res = residual(
        utterances,
        info,
        dense_input.reshape(rows, -1),
        branch.reshape(rows, channels),
        upstream,
        came_all[blocks - 3],
        came_all[blocks - 2],
        came_up,
        gains[blocks],
        width,
    )
    branch_grad = branch_grad.reshape(branch.shape)
    up, hidden_near, grad_res = lax.optimization_barrier((up, hidden_near, grad_res))
    hidden_all.append(gather_hidden(hidden_near, blocks - 1))

    parts = [None] * blocks
    near = None
    for s in range(blocks - 1, -1, -1):
        weight, layer = layers[s]
        if s == 0 and near is not None:
            up, near = lax.optimization_barrier((up, near))
        if s + 2 < blocks:
            up, parts[s + 2] = lax.optimization_barrier((up, parts[s + 2]))
            parts[s + 2] = sum_over_z(parts[s + 2], s + 2)
        before = (None,) * 4
        table, split, _ = plan_grad(s)
        if s > 0:
            before = (turned_all[s - 1], came_all[s - 1], gains[s - 1], biases[s - 1])
        grad, up, sums, low_out, high_out, total = backward_conv(
            utterances, info, up, turned_all[s], low_up, high_up, *edges_all[s], came_all[s], came_up,
            gains[s], *before, weight, layer, copies, split, table,
        )
        gain_grads[s], bias_grads[s] = total[:, :channels], total[:, channels:]
        if near is not None and s > 0:
            sums, near = lax.optimization_barrier((sums, near))
            if s + 2 == blocks:
                near, grad_res, hidden_all = lax.optimization_barrier((near, grad_res, hidden_all))
                grad_res = lax.psum_scatter(grad_res, TIME, scatter_dimension=0, tiled=True)[0]
        elif near is not None:
            up, near = lax.optimization_barrier((up, near))
        if s > 0:
            low_up, high_up = swap_edges(low_out, high_out)
            came_up = every(sums)
            far = None if near is None else other_core(near)
            grad, came_up, low_up, high_up, near, far = lax.optimization_barrier(
                (grad, came_up, low_up, high_up, near, far)
            )
        elif near is not None:
            far = other_core(near)
        if near is not None:
            parts[s + 1] = grad_of_weights(hidden_all[s + 1], near, far, s + 1)
        near = spread_grad(grad, s)
    grad_dense = (
        jnp.einsum("utc,dc->utd", branch_grad, w_res, preferred_element_type=jnp.float32) * valid
    )
    near, parts[1], grad_res, grad_dense = lax.optimization_barrier((near, parts[1], grad_res, grad_dense))
    grad_res = grad_res.reshape(high_z * low_z * inner, cols, -1)
    grad_res = lax.all_to_all(grad_res, BATCH, split_axis=0, concat_axis=0, tiled=True)
    grad_res = jnp.sum(grad_res.astype(jnp.float32), axis=0)
    parts[0] = grad_of_weights(hidden_all[0], near, other_core(near), 0)
    parts[1] = sum_over_z(parts[1], 1)
    parts[0] = sum_over_z_by_pairs(parts[0])
    turned = in_channels // width % LANES == 0
    grad_first = finish(taps, parts[0], turned=turned)[0]
    grad_first = grad_first.transpose(0, 2, 1) if turned else grad_first
    grad_rest = None
    for s in range(blocks - 1, 0, -1):
        grad_rest = finish(taps, parts[s], s - 1, blocks - 1, grad_rest)
    grad_features = up.reshape(features.shape)

    return (
        result.reshape(cotangent.shape),
        grad_features,
        grad_dense,
        grad_first,
        grad_rest,
        grad_res.T,
        jnp.concatenate(gain_grads, axis=0),
        jnp.concatenate(bias_grads, axis=0),
    )


def solution(mesh):
    batch, tm = mesh.shape["batch"], mesh.shape["tm"]
    side = math.isqrt(batch // 2)
    side = side if batch % max(side, 1) == 0 else 1
    deep = batch // side
    low = 2 if deep % 2 == 0 else 1
    cores = 2 if tm % 2 == 0 else 1
    cut = Mesh(mesh.devices.reshape(deep // low, low, side, tm // cores, cores), ALL)
    rows = P(BATCH, TIME, None)
    placed = (rows, rows, P(BATCH), P(BATCH, None), P(BATCH, None))
    placed += (P(), P(), P(), P(), P(), rows)
    return jax.shard_map(
        body,
        mesh=cut,
        in_specs=placed,
        out_specs=(
            rows,
            rows,
            rows,
            P(None, TIME, BATCH),
            P(None, None, TIME, BATCH),
            P(TIME, BATCH),
            P(),
            P(),
        ),
        check_vma=False,
    )
```

```python
import functools
import math

import jax
import jax.numpy as jnp
from jax import lax
from jax.experimental import pallas as pl
from jax.experimental.pallas import tpu as pltpu
from jax.sharding import Mesh, PartitionSpec as P

EPSILON = 1e-05
ALL = ("zh", "zl", "y", "x", "core")
DEPTH = ("zh", "zl")
BATCH = ("zh", "zl", "y")
TIME = ("x", "core")
LANES = 128
GROUP = 7
VMEM = pl.BlockSpec(memory_space=pltpu.VMEM)
SMEM = pl.BlockSpec(memory_space=pltpu.SMEM)
ANY = pl.BlockSpec(memory_space=pl.ANY)
PARAMS = pltpu.CompilerParams(vmem_limit_bytes=60 * 1024 * 1024)


def pieces_of(count):
    return -(-count // (8 * LANES)) * 8


def silu_slope(hidden):
    logistic = jax.nn.sigmoid(hidden)
    return logistic * (1.0 + hidden * (1.0 - logistic))


def plan(utterances, rows, kernel_len):
    phases = rows // LANES
    half = kernel_len // 2
    blocks = []
    for q in range(phases + kernel_len - 1):
        move = (q - half) // phases
        blocks.append((q - half - move * phases, move))
    reach = max(abs(move) for _, move in blocks)
    edge = -(-reach * utterances // 8) * 8
    return phases, blocks, edge


def valid_of(info, utterances, phases, phase, first, shape, axis):
    row = lax.broadcasted_iota(jnp.int32, shape, axis) + first
    frame = info[utterances] + (row // utterances) * phases + phase
    which = row % utterances
    length = jnp.full(shape, info[0], jnp.int32)
    for u in range(1, utterances):
        length = jnp.where(which == u, info[u], length)
    return ((frame >= 0) & (frame < length)).astype(jnp.float32)


def spread_blocks(blocks, utterances, axis, own, edges, put):
    for q, (phase, move) in enumerate(blocks):
        block = own[phase]
        if move:
            spot = lax.broadcasted_iota(jnp.int32, block.shape, axis)
            if move > 0:
                outside = spot < move * utterances
            else:
                outside = spot >= LANES + move * utterances
            block = jnp.where(outside, edges[phase], block)
            block = pltpu.roll(block, (-move * utterances) % LANES, axis)
        put(q, block)


def fetch(weight, base, buffer, sems, g):
    return pltpu.make_async_copy(weight.at[base + g], buffer.at[g], sems.at[g])


def flat_sums(came):
    summed = jnp.sum(came, axis=0)
    return jnp.concatenate([summed[i : i + 1] for i in range(summed.shape[0])], axis=1)


def put_sums(sums, rows_list):
    copies, pieces, _ = sums.shape
    at = 0
    for row in rows_list:
        for i in range(row.shape[1] // LANES):
            piece = row[:, i * LANES : (i + 1) * LANES]
            sums[:, at, :] = jnp.broadcast_to(piece, (copies, LANES))
            at += 1
    if at < pieces:
        sums[:, at:, :] = jnp.zeros((copies, pieces - at, LANES), jnp.float32)


def norm_terms(came, cout):
    summed = flat_sums(came)
    counted = summed[:, 2 * cout : 2 * cout + 1]
    average = summed[:, :cout] / counted
    inv = lax.rsqrt(summed[:, cout : 2 * cout] / counted - average * average + EPSILON)
    return average, inv, counted


def span_of(info, utterances, phases, phase, which, shape):
    at = utterances + 2 + 4 * which
    frame = info[utterances] + lax.broadcasted_iota(jnp.int32, shape, 0) * phases + phase
    channel = lax.broadcasted_iota(jnp.int32, shape, 1)
    inside = (frame >= info[at]) & (frame < info[at] + info[at + 1])
    inside |= (channel >= info[at + 2]) & (channel < info[at + 2] + info[at + 3])
    return ((frame < info[which]) & jnp.logical_not(inside)).astype(jnp.float32)


def frames_of(utterances, phases, phase, which):
    count = LANES // utterances
    return pl.ds(which * count * phases + phase, count, stride=phases)


def rows_of(utterances, first, which):
    return pl.ds(first + which, LANES // utterances, stride=utterances)


def lay(ref, stage):
    for j in range(stage.shape[0]):
        stage[j] = ref[:, j * LANES : (j + 1) * LANES]


def unlay(stage, ref):
    for j in range(stage.shape[0]):
        ref[:, j * LANES : (j + 1) * LANES] = stage[j]


def take(stage, index):
    return jnp.concatenate([stage[j, index, :] for j in range(stage.shape[0])], axis=1)


def give(stage, index, value):
    for j in range(stage.shape[0]):
        stage[j, index, :] = value[:, j * LANES : (j + 1) * LANES]


def forward_kernel(
    cfg, info, source, low, high, came, gain, bias, more, weight, linear, sums, low_out, high_out, flat, turned,
    buffer, haloed, sems, laid, staged,
):
    utterances, phases, blocks, edge, taps, base, normed = cfg
    groups = taps // GROUP
    rows, cin = source.shape
    cout = linear.shape[1]
    fetch(weight, base, buffer, sems, 0).start()
    if normed:
        average, inv, _ = norm_terms(came[...], cin)
        scale = inv * gain[...]
        shift = bias[...] - average * scale

    else:
        lay(source, laid)

    def activate(value, mask):
        if not normed:
            return value.astype(jnp.float32)
        value = value * scale + shift
        return value * jax.nn.sigmoid(value) * mask

    own, edges = [], []
    for p in range(phases):
        if normed:
            mask = valid_of(info, utterances, phases, p, 0, (LANES, 1), 0)
            block = activate(source[p * LANES : (p + 1) * LANES, :], mask).astype(jnp.bfloat16)
        else:
            for u in range(utterances):
                mask = span_of(info, utterances, phases, p, u, (LANES // utterances, cin))
                give(staged, rows_of(utterances, 0, u), take(laid, frames_of(utterances, phases, p, u)) * mask)
            block = take(staged, slice(None)).astype(jnp.bfloat16)
        own.append(block)
        flat[:, p * LANES : (p + 1) * LANES] = block.T
        mask = valid_of(info, utterances, phases, p, -edge, (edge, 1), 0)
        before = activate(low[p], mask)
        mask = valid_of(info, utterances, phases, p, LANES, (edge, 1), 0)
        after = activate(high[p], mask)
        middle = jnp.zeros((LANES - 2 * edge, cin), jnp.float32)
        edges.append(jnp.concatenate([after, middle, before], axis=0).astype(jnp.bfloat16))

    def put(q, block):
        haloed[q * LANES : (q + 1) * LANES, :] = block

    if groups > 1:
        fetch(weight, base, buffer, sems, 1).start()
    spread_blocks(blocks, utterances, 0, own, edges, put)
    linear[...] = jnp.zeros_like(linear)

    def step(g, carry):
        fetch(weight, base, buffer, sems, g).wait()

        @pl.when(g + 2 < groups)
        def _():
            fetch(weight, base, buffer, sems, g + 2).start()

        lhs = jnp.concatenate(
            [
                haloed[pl.ds(pl.multiple_of((g * GROUP + k) * LANES, LANES), rows), :]
                for k in range(GROUP)
            ],
            axis=1,
        )
        linear[...] += jnp.dot(lhs, buffer[g], preferred_element_type=jnp.float32)
        return carry

    lax.fori_loop(0, groups, step, 0)
    total = jnp.zeros((1, cout), jnp.float32)
    square = jnp.zeros((1, cout), jnp.float32)
    count = jnp.zeros((1, 1), jnp.float32)
    for p in range(phases):
        mask = valid_of(info, utterances, phases, p, 0, (LANES, 1), 0)
        block = linear[p * LANES : (p + 1) * LANES, :]
        masked = block * mask
        total += jnp.sum(masked, axis=0, keepdims=True)
        square += jnp.sum(masked * block, axis=0, keepdims=True)
        count += jnp.sum(mask, axis=0, keepdims=True)
        low_out[p] = block[LANES - edge :, :]
        high_out[p] = block[:edge, :]
        turned[:, p * LANES : (p + 1) * LANES] = block.astype(jnp.bfloat16).T
    terms = [total, square, jnp.broadcast_to(count, (1, LANES))]
    if more is not None:
        terms.append(more[...])
    put_sums(sums, terms)


def forward_conv(utterances, info, source, low, high, came, gain, bias, weight, layer, copies, more=None):
    _, taps, cin, cout = weight.shape
    rows = source.shape[0]
    phases, blocks, edge = plan(utterances, rows, taps)
    groups = taps // GROUP
    normed = came is not None
    if not normed:
        came = jnp.zeros((1, 8, LANES), jnp.float32)
        gain = bias = jnp.zeros((1, LANES), jnp.float32)
    cfg = (utterances, phases, blocks, edge, taps, layer * groups, normed)
    shape = jax.ShapeDtypeStruct
    terms = 2 * cout + LANES
    kernel = functools.partial(forward_kernel, cfg)
    extra = []
    if more is None:
        kernel = lambda *refs: forward_kernel(cfg, *refs[:7], None, *refs[7:])
    else:
        terms += more.shape[1]
        extra = [more]
    return pl.pallas_call(
        kernel,
        name="forward_conv",
        out_shape=(
            shape((rows, cout), jnp.float32),
            shape((copies, pieces_of(terms), LANES), jnp.float32),
            shape((phases, edge, cout), jnp.float32),
            shape((phases, edge, cout), jnp.float32),
            shape((cin, rows), jnp.bfloat16),
            shape((cout, rows), jnp.bfloat16),
        ),
        in_specs=[SMEM] + [VMEM] * (6 + len(extra)) + [ANY],
        out_specs=(VMEM,) * 6,
        scratch_shapes=[
            pltpu.VMEM((groups, GROUP * cin, cout), jnp.bfloat16),
            pltpu.VMEM((len(blocks) * LANES, cin), jnp.bfloat16),
            pltpu.SemaphoreType.DMA((groups,)),
            pltpu.VMEM((1 if normed else cin // LANES, 8 if normed else rows, LANES), jnp.float32),
            pltpu.VMEM((cin // LANES, LANES, LANES), jnp.float32),
        ],
        compiler_params=PARAMS,
        cost_estimate=pl.CostEstimate(
            flops=2 * taps * rows * cin * cout, bytes_accessed=2 * taps * cin * cout, transcendentals=0
        ),
    )(info, source, low, high, came, gain, bias, *extra, weight.reshape(-1, GROUP * cin, cout))


def columns_of(rows_list):
    count = len(rows_list)
    width = rows_list[0].shape[1]
    stacked = jnp.concatenate(
        rows_list + [jnp.zeros((LANES - count, width), jnp.float32)], axis=0
    )
    return stacked.T


def put_grad(out, value, table):
    if len(out.shape) == 2:
        out[...] = value
        return
    cols = out.shape[3]
    for g, blocks in enumerate(table):
        for k, block in enumerate(blocks):
            for x in range(out.shape[1]):
                out[g, x, k] = value[block * cols : (block + 1) * cols]


def backward_kernel(
    cfg, info, up, linear, low_up, high_up, low_lin, high_lin, came, came_up, gain, before, came_before,
    gain_before, bias_before, weight, grad, next_up, sums, low_out, high_out, row, buffer, haloed, sems, staged,
    whole, laid,
):
    utterances, phases, blocks, edge, taps, base, last, table = cfg
    groups = taps // GROUP
    cout, rows = up.shape
    cin = weight.shape[2]
    fetch(weight, base, buffer, sems, 0).start()
    average, inv, counted = norm_terms(came[...], cout)
    summed = flat_sums(came_up[...])
    grad_gain, grad_bias = summed[:, :cout], summed[:, cout : 2 * cout]
    row[...] = summed[:, : 2 * cout]
    keep_up = gain[...] * inv
    keep_lin = -keep_up * inv * grad_gain / counted
    rest = -keep_up * grad_bias / counted - keep_lin * average
    vectors = [keep_up, keep_lin, rest]
    if not last:
        average_b, inv_b, _ = norm_terms(came_before[...], cin)
        scale = inv_b * gain_before[...]
        vectors += [scale, bias_before[...] - average_b * scale, inv_b, -average_b * inv_b]
    columns = columns_of(vectors)

    def column(r):
        return columns[:, r : r + 1]

    pieces = []
    for p in range(phases):
        for first, up_edge, lin_edge in ((-edge, low_up, low_lin), (LANES, high_up, high_lin)):
            mask = valid_of(info, utterances, phases, p, first, (edge, 1), 0)
            pieces.append(mask * (up_edge[p] * keep_up + lin_edge[p] * keep_lin + rest))
    pieces.append(jnp.zeros((LANES - 2 * phases * edge, cout), jnp.float32))
    side = jnp.concatenate(pieces, axis=0).T
    own, edges, grads = [], [], []
    spot = lax.broadcasted_iota(jnp.int32, (cout, LANES), 1)
    for p in range(phases):
        cut = slice(p * LANES, (p + 1) * LANES)
        mask = valid_of(info, utterances, phases, p, 0, (1, LANES), 1)
        block = mask * (up[:, cut] * column(0) + linear[:, cut].astype(jnp.float32) * column(1) + column(2))
        block = block.astype(jnp.bfloat16)
        own.append(block)
        grads.append(block)
        at = 2 * p * edge
        after = pltpu.roll(side, (-(at + edge)) % LANES, 1)
        ahead = pltpu.roll(side, (LANES - edge - at) % LANES, 1)
        edges.append(jnp.where(spot < edge, after, ahead).astype(jnp.bfloat16))

    put_grad(grad, jnp.concatenate(grads, axis=1), table)

    def put(q, block):
        haloed[:, q * LANES : (q + 1) * LANES] = block

    if groups > 1:
        fetch(weight, base, buffer, sems, 1).start()
    spread_blocks(blocks, utterances, 1, own, edges, put)
    total = whole if last else next_up
    for g in range(groups):
        fetch(weight, base, buffer, sems, g).wait()
        if g + 2 < groups:
            fetch(weight, base, buffer, sems, g + 2).start()
        lhs = jnp.concatenate([buffer[g, k] for k in range(GROUP)], axis=1)
        starts = [(taps - 1 - g * GROUP - k) * LANES for k in range(GROUP)]
        rhs = jnp.concatenate([haloed[:, at : at + rows] for at in starts], axis=0)
        product = jnp.dot(lhs, rhs, preferred_element_type=jnp.float32)
        total[...] = product if g == 0 else total[...] + product
    if last:
        for p in range(phases):
            give(staged, slice(None), total[:, p * LANES : (p + 1) * LANES].T)
            for u in range(utterances):
                mask = span_of(info, utterances, phases, p, u, (LANES // utterances, cin))
                give(laid, frames_of(utterances, phases, p, u), take(staged, rows_of(utterances, 0, u)) * mask)
        unlay(laid, next_up)
        return
    gains = jnp.zeros((cin, LANES), jnp.float32)
    biases = jnp.zeros((cin, LANES), jnp.float32)
    ends = jnp.zeros((cin, LANES), jnp.float32)
    spot = lax.broadcasted_iota(jnp.int32, (cin, LANES), 1)
    for p in range(phases):
        cut = slice(p * LANES, (p + 1) * LANES)
        mask = valid_of(info, utterances, phases, p, 0, (1, LANES), 1)
        value = before[:, cut].astype(jnp.float32)
        block = next_up[:, cut] * mask * silu_slope(value * column(3) + column(4))
        next_up[:, cut] = block
        gains += block * (value * column(5) + column(6))
        biases += block
        at = 2 * p * edge
        rolled = pltpu.roll(block, (at + edge) % LANES, 1)
        ends = jnp.where((spot >= at) & (spot < at + 2 * edge), rolled, ends)
    ends = ends.T
    for p in range(phases):
        at = 2 * p * edge
        low_out[p] = ends[at : at + edge, :]
        high_out[p] = ends[at + edge : at + 2 * edge, :]
    gains = jnp.sum(gains.T, axis=0, keepdims=True)
    biases = jnp.sum(biases.T, axis=0, keepdims=True)
    put_sums(sums, [gains, biases])


def backward_conv(
    utterances, info, up, linear, low_up, high_up, low_lin, high_lin, came, came_up, gain, before, came_before,
    gain_before, bias_before, weight, layer, copies, split, table,
):
    _, taps, cin, cout = weight.shape
    rows = up.shape[1]
    phases, blocks, edge = plan(utterances, rows, taps)
    groups = taps // GROUP
    last = before is None
    if last:
        before = jnp.zeros((16, LANES), jnp.bfloat16)
        came_before = jnp.zeros((1, 8, LANES), jnp.float32)
        gain_before = bias_before = jnp.zeros((1, LANES), jnp.float32)
    shape = jax.ShapeDtypeStruct
    cfg = (utterances, phases, blocks, edge, taps, layer * groups, last, table)
    return pl.pallas_call(
        functools.partial(backward_kernel, cfg),
        name="backward_conv",
        out_shape=(
            shape(split + (rows,), jnp.bfloat16),
            shape((rows, cin) if last else (cin, rows), jnp.float32),
            shape((copies, pieces_of(2 * cin), LANES), jnp.float32),
            shape((phases, edge, cin), jnp.float32),
            shape((phases, edge, cin), jnp.float32),
            shape((1, 2 * cout), jnp.float32),
        ),
        in_specs=[SMEM] + [VMEM] * 13 + [ANY],
        out_specs=(VMEM,) * 6,
        scratch_shapes=[
            pltpu.VMEM((groups, GROUP, cin, cout), jnp.bfloat16),
            pltpu.VMEM((cout, len(blocks) * LANES), jnp.bfloat16),
            pltpu.SemaphoreType.DMA((groups,)),
            pltpu.VMEM((cin // LANES, LANES, LANES), jnp.float32),
            pltpu.VMEM((cin, rows) if last else (8, LANES), jnp.float32),
            pltpu.VMEM((cin // LANES, rows, LANES) if last else (1, 8, LANES), jnp.float32),
        ],
        compiler_params=PARAMS,
        cost_estimate=pl.CostEstimate(
            flops=2 * taps * rows * cin * cout, bytes_accessed=2 * taps * cin * cout, transcendentals=0
        ),
    )(
        info, up, linear, low_up, high_up, low_lin, high_lin, came, came_up, gain, before, came_before,
        gain_before, bias_before, weight.reshape(-1, GROUP, cin, cout),
    )


def weight_kernel(cfg, info, hidden_all, *refs):
    utterances, phases, blocks, taps, batch, first, parts = cfg
    pieces, (out, hidden, grad, haloed, total, sems) = refs[:parts], refs[parts:]
    inner, width, cin, rows = hidden.shape
    cout = grad.shape[2]
    across = width // parts

    def copies_of(b):
        for p, piece in enumerate(pieces):
            for x in range(across):
                at = (p * inner + b) * across + x
                yield pltpu.make_async_copy(piece.at[b * across + x], grad.at[at], sems.at[at])
        source = hidden_all.at[b, :, pl.ds(first, cin), :]
        yield pltpu.make_async_copy(source, hidden.at[b], sems.at[width * inner + b])

    def start(b, carry):
        for copy in copies_of(b):
            copy.start()
        return carry

    lax.fori_loop(0, inner, start, 0)
    zero = jnp.zeros((cin, LANES), hidden.dtype)
    spot = lax.broadcasted_iota(jnp.int32, (cin, LANES), 1)

    def unit(b):
        for copy in copies_of(b):
            copy.wait()
        for t in range(width):
            for q, (phase, move) in enumerate(blocks):
                cut = slice(phase * LANES, (phase + 1) * LANES)
                block = hidden[b, t, :, cut]
                if move:
                    if move > 0:
                        other = hidden[b, t + 1, :, cut] if t + 1 < width else zero
                        outside = spot < move * utterances
                    else:
                        other = hidden[b, t - 1, :, cut] if t > 0 else zero
                        outside = spot >= LANES + move * utterances
                    block = pltpu.roll(jnp.where(outside, other, block), (-move * utterances) % LANES, 1)
                haloed[t, :, q * LANES : (q + 1) * LANES] = block
        lhs = jnp.concatenate(
            [grad[(p * inner + b) * across + x] for p in range(parts) for x in range(across)], axis=1
        )

        places = [x * parts + jnp.bitwise_xor(info[0], p) for p in range(parts) for x in range(across)]
        for g in range(taps // batch):
            rhs = jnp.concatenate(
                [
                    jnp.concatenate([haloed[place, :, k * LANES : k * LANES + rows] for place in places], axis=1)
                    for k in range(g * batch, (g + 1) * batch)
                ],
                axis=0,
            )
            product = lax.dot_general(
                lhs, rhs, (((1,), (1,)), ((), ())), preferred_element_type=jnp.float32
            )
            total[g] = product if b == 0 else total[g] + product

    for b in range(inner):
        unit(b)
    outer, _, cols, _ = out.shape
    for z in range(outer):
        out[z] = total[:, z * cols : (z + 1) * cols, :].astype(jnp.bfloat16)


def weight_grad(utterances, taps, order, hidden, first, cin, grad, outer):
    inner, width, _, rows = hidden.shape
    cout = grad[0].shape[1]
    phases, blocks, _ = plan(utterances, rows, taps)
    batch = 7
    cfg = (utterances, phases, blocks, taps, batch, first, len(grad))
    return pl.pallas_call(
        functools.partial(weight_kernel, cfg),
        name="weight_grad",
        out_shape=jax.ShapeDtypeStruct((outer, taps // batch, cout // outer, batch * cin), jnp.bfloat16),
        in_specs=[SMEM] + [ANY] * (1 + len(grad)),
        out_specs=VMEM,
        scratch_shapes=[
            pltpu.VMEM((inner, width, cin, rows), jnp.bfloat16),
            pltpu.VMEM((width * inner, cout, rows), jnp.bfloat16),
            pltpu.VMEM((width, cin, len(blocks) * LANES), jnp.bfloat16),
            pltpu.VMEM((taps // batch, cout, batch * cin), jnp.float32),
            pltpu.SemaphoreType.DMA((inner + width * inner,)),
        ],
        compiler_params=PARAMS,
        cost_estimate=pl.CostEstimate(
            flops=2 * taps * inner * width * rows * cin * cout,
            bytes_accessed=2 * inner * width * rows * (cin + cout),
            transcendentals=0,
        ),
    )(order, hidden, *grad)


def branch_terms(first, second, counted, channels):
    at = 2 * channels + LANES
    average = flat_sums(first[...])[:, at : at + channels] / counted
    square = flat_sums(second[...])[:, at : at + channels] / counted
    return average, lax.rsqrt(square - average * average + EPSILON)


def middle_kernel(
    cfg, info, linear, came, first, second, branch, cotangent, gain, bias, branch_gain, branch_bias, result, up, turned, sums,
    low_out, high_out, staged, linear_laid, branch_laid, cotangent_laid, result_laid, up_laid,
):
    utterances, phases, edge = cfg
    channels = linear.shape[1]
    average, inv, counted = norm_terms(came[...], channels)
    branch_average, branch_inv = branch_terms(first, second, counted, channels)
    zero = jnp.zeros((1, channels), jnp.float32)
    gain_sum, bias_sum, branch_sum = zero, zero, zero
    lay(linear, linear_laid)
    lay(branch, branch_laid)
    lay(cotangent, cotangent_laid)
    shape = (LANES // utterances, 1)
    for p in range(phases):
        for u in range(utterances):
            here = frames_of(utterances, phases, p, u)
            frame = info[utterances] + lax.broadcasted_iota(jnp.int32, shape, 0) * phases + p
            mask = (frame < info[u]).astype(jnp.float32)
            scaled = (take(linear_laid, rows_of(utterances, p * LANES, u)) - average) * inv
            branch_scaled = (take(branch_laid, here) - branch_average) * branch_inv
            joined = scaled * gain[...] + bias[...] + (branch_scaled * branch_gain[...] + branch_bias[...])
            logistic = jax.nn.sigmoid(joined)
            give(result_laid, here, joined * logistic * mask)
            grad = take(cotangent_laid, here) * mask * (logistic * (1.0 + joined * (1.0 - logistic)))
            give(up_laid, here, grad)
            give(staged, rows_of(utterances, 0, u), grad)
            gain_sum += jnp.sum(grad * scaled, axis=0, keepdims=True)
            bias_sum += jnp.sum(grad, axis=0, keepdims=True)
            branch_sum += jnp.sum(grad * branch_scaled, axis=0, keepdims=True)
        block = take(staged, slice(None))
        turned[:, p * LANES : (p + 1) * LANES] = block.T
        low_out[p] = block[LANES - edge :, :]
        high_out[p] = block[:edge, :]
    unlay(result_laid, result)
    unlay(up_laid, up)
    put_sums(sums, [gain_sum, bias_sum, branch_sum])


def middle(utterances, info, linear, came, first, second, branch, cotangent, terms, edge, copies):
    rows, channels = linear.shape
    phases = rows // LANES
    shape = jax.ShapeDtypeStruct
    return pl.pallas_call(
        functools.partial(middle_kernel, (utterances, phases, edge)),
        name="middle",
        out_shape=(
            shape((rows, channels), jnp.float32),
            shape((rows, channels), jnp.float32),
            shape((channels, rows), jnp.float32),
            shape((copies, pieces_of(3 * channels), LANES), jnp.float32),
            shape((phases, edge, channels), jnp.float32),
            shape((phases, edge, channels), jnp.float32),
        ),
        in_specs=[SMEM] + [VMEM] * 10,
        out_specs=(VMEM,) * 6,
        scratch_shapes=[pltpu.VMEM((channels // LANES, LANES, LANES), jnp.float32)]
        + [pltpu.VMEM((channels // LANES, rows, LANES), jnp.float32)] * 5,
        compiler_params=PARAMS,
        cost_estimate=pl.CostEstimate(
            flops=40 * rows * channels, bytes_accessed=24 * rows * channels, transcendentals=rows * channels
        ),
    )(info, linear, came, first, second, branch, cotangent, *terms)


def residual_kernel(cfg, info, dense, branch, up, first, second, came_up, gain, grad, product):
    utterances, parts = cfg
    rows, channels = branch.shape
    total = flat_sums(came_up[...])
    counted = flat_sums(first[...])[:, 2 * channels : 2 * channels + 1]
    average, inv = branch_terms(first, second, counted, channels)
    keep_up = gain[...] * inv
    keep_branch = -keep_up * inv * total[:, 2 * channels : 3 * channels] / counted
    rest = -keep_up * total[:, channels : 2 * channels] / counted - keep_branch * average
    count = rows // utterances
    frame = info[utterances] + lax.broadcasted_iota(jnp.int32, (count, 1), 0)
    mask = jnp.concatenate([(frame < info[u]).astype(jnp.float32) for u in range(utterances)], axis=0)
    value = (mask * (up[...] * keep_up + branch[...] * keep_branch + rest)).astype(jnp.bfloat16)
    grad[...] = value
    turned = value.T
    size = dense.shape[1] // parts
    if size % LANES == 0:
        for t in range(parts):
            low = (dense[:, t * size : (t + 1) * size] * mask).astype(jnp.bfloat16)
            product[t] = jnp.dot(turned, low, preferred_element_type=jnp.float32).astype(jnp.bfloat16)
    else:
        low = (dense[...] * mask).astype(jnp.bfloat16)
        every_part = jnp.dot(turned, low, preferred_element_type=jnp.float32).astype(jnp.bfloat16)
        for t in range(parts):
            product[t] = every_part[:, t * size : (t + 1) * size]


def residual(utterances, info, dense, branch, up, first, second, came_up, gain, parts):
    rows, channels = branch.shape
    deep = dense.shape[1]
    shape = jax.ShapeDtypeStruct
    return pl.pallas_call(
        functools.partial(residual_kernel, (utterances, parts)),
        name="residual",
        out_shape=(
            shape((rows, channels), jnp.bfloat16),
            shape((parts, channels, deep // parts), jnp.bfloat16),
        ),
        in_specs=[SMEM] + [VMEM] * 7,
        out_specs=(VMEM,) * 2,
        compiler_params=PARAMS,
        cost_estimate=pl.CostEstimate(
            flops=2 * rows * channels * deep, bytes_accessed=4 * rows * deep, transcendentals=0
        ),
    )(info, dense, branch, up, first, second, came_up, gain)


def finish_kernel(cfg, *refs):
    taps, terms, turned = cfg
    parts, out = refs[:terms], refs[-1]
    groups = parts[0].shape[0]
    batch = taps // groups
    for g in range(groups):
        block = parts[0][g].astype(jnp.float32)
        for part in parts[1:]:
            block += part[g].astype(jnp.float32)
        size = block.shape[1] // batch
        if turned:
            for k in range(batch):
                out[g * batch + k] = block[:, k * size : (k + 1) * size]
        else:
            out[g * batch : (g + 1) * batch] = block.T.reshape(batch, size, block.shape[0])


def finish(taps, parts, layer=0, layers=1, buffer=None, turned=False):
    groups, cols, long = parts[0].shape
    cin = long * groups // taps
    block = (taps, cols, cin) if turned else (taps, cin, cols)
    extra = [] if buffer is None else [buffer]
    return pl.pallas_call(
        functools.partial(finish_kernel, (taps, len(parts), turned)),
        name="finish",
        grid=(1,),
        out_shape=jax.ShapeDtypeStruct((layers,) + block, jnp.float32),
        in_specs=[VMEM] * len(parts) + [ANY] * len(extra),
        out_specs=pl.BlockSpec((None,) + block, lambda i: (layer, 0, 0, 0)),
        input_output_aliases={len(parts): 0} if extra else {},
        compiler_params=PARAMS,
    )(*parts, *extra)


def span_keep(span_cols, positions):
    inside = (positions[None, :] >= span_cols[:, 0:1]) & (
        positions[None, :] < span_cols[:, 0:1] + span_cols[:, 1:2]
    )
    return 1.0 - inside.astype(jnp.float32)


def edge_rows(frames, phases):
    utterances, count, channels = frames.shape
    cut = frames.reshape(utterances, count // phases, phases, channels).transpose(2, 1, 0, 3)
    return cut.reshape(phases, utterances * count // phases, channels)


def swap_edges(low_out, high_out):
    count = lax.axis_size(TIME)
    low = lax.ppermute(low_out, TIME, [(i, i + 1) for i in range(count - 1)])
    high = lax.ppermute(high_out, TIME, [(i + 1, i) for i in range(count - 1)])
    return low, high


def every(copies):
    return lax.all_to_all(copies, ALL, split_axis=0, concat_axis=0, tiled=True)


def body(
    features,
    dense_input,
    lengths,
    time_span,
    freq_span,
    w_first,
    w_rest,
    w_res,
    norm_gains,
    norm_biases,
    cotangent,
):
    utterances, frames_here, in_channels = features.shape
    high_z, low_z, inner, across, cores = (lax.axis_size(name) for name in ALL)
    outer = high_z * low_z
    width = across * cores
    copies = outer * inner * width
    taps, _, channels = w_first.shape
    blocks = 1 + w_rest.shape[0]
    rows = utterances * frames_here
    phases, _, edge = plan(utterances, rows, taps)
    cols = channels // (outer * inner)
    late = 0
    whole_table = [[z * inner + y for z in range(outer)] for y in range(inner)]
    half_table = [
        [(h * low_z + l) * inner + y for h in range(high_z)] for l in range(low_z) for y in range(inner)
    ]
    offset = lax.axis_index(TIME) * frames_here
    spans = jnp.concatenate([time_span, freq_span], axis=1).reshape(-1)
    info = jnp.concatenate([lengths, jnp.stack([offset, 0]).astype(jnp.int32), spans])
    frames = offset + jnp.arange(frames_here, dtype=jnp.int32)
    valid = (frames[None, :] < lengths[:, None]).astype(jnp.float32)[:, :, None]
    layers = [(w_first[None], 0)] + [(w_rest, s) for s in range(blocks - 1)]
    gains = [norm_gains[s : s + 1] for s in range(blocks + 1)]
    biases = [norm_biases[s : s + 1] for s in range(blocks + 1)]

    def masked_edge(first, count):
        at = frames[first : first + count]
        keep = (at[None, :] < lengths[:, None]).astype(jnp.float32)[:, :, None]
        keep *= span_keep(time_span, at)[:, :, None]
        keep *= span_keep(freq_span, jnp.arange(in_channels, dtype=jnp.int32))[:, None, :]
        cut = (features[:, first : first + count] * keep).astype(jnp.bfloat16)
        return edge_rows(cut.astype(jnp.float32), phases)

    def spread_hidden(turned):
        cut = turned.reshape(width, turned.shape[0] // width, rows)
        return lax.all_to_all(cut, TIME, split_axis=0, concat_axis=0, tiled=True)

    def gather_hidden(near, s):
        return lax.all_gather(near, "y" if s >= late else ("zl", "y"))

    def plan_grad(s):
        table, axes = (whole_table, ("y",)) if s >= late else (half_table, ("zl", "y"))
        split = (len(table), across, len(table[0]), cols) if cols % 16 == 0 else (channels,)
        return table, split, axes + ("x",)

    def spread_grad(grad, s):
        table, _, axes = plan_grad(s)
        if grad.ndim == 2:
            cut = grad.reshape(outer * inner, cols, rows)[jnp.array(table)][:, None]
            grad = jnp.broadcast_to(cut, (len(table), across) + cut.shape[2:])
        grad = grad.reshape(len(table) * across, -1, rows)
        return lax.all_to_all(grad, axes, split_axis=0, concat_axis=0, tiled=True)

    def other_core(near):
        return lax.ppermute(near, "core", [(0, 1), (1, 0)]) if cores == 2 else None

    def grad_of_weights(hidden, near, far, s):
        pieces, order = [near], jnp.zeros((1,), jnp.int32)
        if far is not None:
            pieces.append(far)
            order = lax.axis_index("core").astype(jnp.int32)[None]
        places = outer if s >= late else high_z
        return weight_grad(utterances, taps, order, hidden, 0, hidden.shape[2], pieces, places)

    def sum_over_z_by_pairs(part):
        if (high_z, low_z) != (2, 2):
            return sum_over_z(part, 0)
        me = 2 * lax.axis_index("zh") + lax.axis_index("zl")

        def block(bits):
            return lax.dynamic_index_in_dim(part, jnp.bitwise_xor(me, bits), 0, keepdims=False)

        across = lax.ppermute(block(3), "zl", [(0, 1), (1, 0)])
        beside = lax.ppermute(block(1), "zl", [(0, 1), (1, 0)])
        both = (block(2).astype(jnp.float32) + across.astype(jnp.float32)).astype(jnp.bfloat16)
        return [block(0), beside, lax.ppermute(both, "zh", [(0, 1), (1, 0)])]

    def sum_over_z(part, s):
        if s >= late:
            return [lax.psum_scatter(part, DEPTH, scatter_dimension=0, tiled=True)[0]]
        if high_z != 2:
            return [lax.psum_scatter(part, "zh", scatter_dimension=0, tiled=True)[0]]
        me = lax.axis_index("zh")
        away = lax.dynamic_index_in_dim(part, 1 - me, 0, keepdims=False)
        came = lax.ppermute(away, "zh", [(0, 1), (1, 0)])
        own = lax.dynamic_index_in_dim(part, me, 0, keepdims=False)
        return [own, came]

    reach = edge * phases // utterances
    low, high = swap_edges(masked_edge(frames_here - reach, reach), masked_edge(0, reach))
    source = features.reshape(rows, in_channels)
    dense_low = (dense_input * valid).astype(jnp.bfloat16)
    branch = jnp.einsum("utd,dc->utc", dense_low, w_res, preferred_element_type=jnp.float32)
    branch_sums = {
        blocks - 3: jnp.sum(branch * valid, axis=(0, 1))[None],
        blocks - 2: jnp.sum(branch * branch * valid, axis=(0, 1))[None],
    }
    came_all, hidden_all, turned_all, edges_all = [], [], [], []
    came = None
    near = None
    for s in range(blocks):
        weight, layer = layers[s]
        more = branch_sums.get(s)
        source, sums, low_out, high_out, flat, turned = forward_conv(
            utterances, info, source, low, high, came, gains[s - 1], biases[s - 1], weight, layer, copies, more
        )
        if near is not None:
            done = hidden_all[: max(s - 2, 0)]
            sums, near, done = lax.optimization_barrier((sums, near, done))
            hidden_all[: len(done)] = done
            hidden_all.append(gather_hidden(near, s - 1))
        low, high = swap_edges(low_out, high_out)
        came = every(sums)
        flat, came, low, high = lax.optimization_barrier((flat, came, low, high))
        if s + 1 < blocks:
            near = spread_hidden(flat)
        came_all.append(came)
        turned_all.append(turned)
        edges_all.append((low, high))

    result, upstream, up, sums, low_out, high_out = middle(
        utterances,
        info,
        source,
        came,
        came_all[blocks - 3],
        came_all[blocks - 2],
        branch.reshape(rows, channels),
        cotangent.reshape(rows, channels),
        (gains[blocks - 1], biases[blocks - 1], gains[blocks], biases[blocks]),
        edge,
        copies,
    )
    done = hidden_all[: blocks - 2]
    sums, done = lax.optimization_barrier((sums, done))
    hidden_all[: len(done)] = done
    low_up, high_up = swap_edges(low_out, high_out)
    came_up = every(sums)
    flat, came_up, low_up, high_up = lax.optimization_barrier((flat, came_up, low_up, high_up))
    hidden_near = spread_hidden(flat)

    def row_of(terms):
        return jnp.sum(terms, axis=0).reshape(1, -1)

    total = row_of(came_up)
    gain_grads, bias_grads = [None] * (blocks + 1), [None] * (blocks + 1)
    gain_grads[blocks], bias_grads[blocks] = total[:, 2 * channels : 3 * channels], total[:, channels : 2 * channels]
    branch_grad, grad_res = residual(
        utterances,
        info,
        dense_input.reshape(rows, -1),
        branch.reshape(rows, channels),
        upstream,
        came_all[blocks - 3],
        came_all[blocks - 2],
        came_up,
        gains[blocks],
        width,
    )
    branch_grad = branch_grad.reshape(branch.shape)
    up, hidden_near, grad_res = lax.optimization_barrier((up, hidden_near, grad_res))
    hidden_all.append(gather_hidden(hidden_near, blocks - 1))

    parts = [None] * blocks
    near = None
    for s in range(blocks - 1, -1, -1):
        weight, layer = layers[s]
        if s == 0 and near is not None:
            up, near = lax.optimization_barrier((up, near))
        if s + 2 < blocks:
            up, parts[s + 2] = lax.optimization_barrier((up, parts[s + 2]))
            parts[s + 2] = sum_over_z(parts[s + 2], s + 2)
        before = (None,) * 4
        table, split, _ = plan_grad(s)
        if s > 0:
            before = (turned_all[s - 1], came_all[s - 1], gains[s - 1], biases[s - 1])
        grad, up, sums, low_out, high_out, total = backward_conv(
            utterances, info, up, turned_all[s], low_up, high_up, *edges_all[s], came_all[s], came_up,
            gains[s], *before, weight, layer, copies, split, table,
        )
        gain_grads[s], bias_grads[s] = total[:, :channels], total[:, channels:]
        if near is not None and s > 0:
            sums, near = lax.optimization_barrier((sums, near))
            if s + 2 == blocks:
                near, grad_res, hidden_all = lax.optimization_barrier((near, grad_res, hidden_all))
                grad_res = lax.psum_scatter(grad_res, TIME, scatter_dimension=0, tiled=True)[0]
        elif near is not None:
            up, near = lax.optimization_barrier((up, near))
        if s > 0:
            low_up, high_up = swap_edges(low_out, high_out)
            came_up = every(sums)
            far = None if near is None else other_core(near)
            grad, came_up, low_up, high_up, near, far = lax.optimization_barrier(
                (grad, came_up, low_up, high_up, near, far)
            )
        elif near is not None:
            far = other_core(near)
        if near is not None:
            parts[s + 1] = grad_of_weights(hidden_all[s + 1], near, far, s + 1)
        near = spread_grad(grad, s)
    grad_dense = (
        jnp.einsum("utc,dc->utd", branch_grad, w_res, preferred_element_type=jnp.float32) * valid
    )
    near, parts[1], grad_res, grad_dense = lax.optimization_barrier((near, parts[1], grad_res, grad_dense))
    grad_res = grad_res.reshape(high_z * low_z * inner, cols, -1)
    grad_res = lax.all_to_all(grad_res, BATCH, split_axis=0, concat_axis=0, tiled=True)
    grad_res = jnp.sum(grad_res.astype(jnp.float32), axis=0)
    parts[0] = grad_of_weights(hidden_all[0], near, other_core(near), 0)
    parts[1] = sum_over_z(parts[1], 1)
    parts[0] = sum_over_z_by_pairs(parts[0])
    turned = in_channels // width % LANES == 0
    grad_first = finish(taps, parts[0], turned=turned)[0]
    grad_first = grad_first.transpose(0, 2, 1) if turned else grad_first
    grad_rest = None
    for s in range(blocks - 1, 0, -1):
        grad_rest = finish(taps, parts[s], s - 1, blocks - 1, grad_rest)
    grad_features = up.reshape(features.shape)

    return (
        result.reshape(cotangent.shape),
        grad_features,
        grad_dense,
        grad_first,
        grad_rest,
        grad_res.T,
        jnp.concatenate(gain_grads, axis=0),
        jnp.concatenate(bias_grads, axis=0),
    )


def solution(mesh):
    batch, tm = mesh.shape["batch"], mesh.shape["tm"]
    side = math.isqrt(batch // 2)
    side = side if batch % max(side, 1) == 0 else 1
    deep = batch // side
    low = 2 if deep % 2 == 0 else 1
    cores = 2 if tm % 2 == 0 else 1
    cut = Mesh(mesh.devices.reshape(deep // low, low, side, tm // cores, cores), ALL)
    rows = P(BATCH, TIME, None)
    placed = (rows, rows, P(BATCH), P(BATCH, None), P(BATCH, None))
    placed += (P(), P(), P(), P(), P(), rows)
    return jax.shard_map(
        body,
        mesh=cut,
        in_specs=placed,
        out_specs=(
            rows,
            rows,
            rows,
            P(None, TIME, BATCH),
            P(None, None, TIME, BATCH),
            P(TIME, BATCH),
            P(),
            P(),
        ),
        check_vma=False,
    )
```
